256 devices in a mesh: seq: 8 (over x, core), exp: 16 (over y, z_lo), dp: 2 (over z_hi).
Axes of the slice: x: 4, y: 4, z: 8 (z_hi: 2, z_lo: 4; z = z_hi * 4 + z_lo), core: 2. Of those that a mesh axis runs over, the one named last changes fastest.
Arguments:
- tokens: bfloat16 [524288, 1280], P(('dp', 'seq', 'exp')), parts along dimension 0, may hold values from -60 to 60
- slot_keys: bfloat16 [1280, 256], replicated, may hold values from -1 to 1
- w_in: bfloat16 [16, 1280, 5120], P('exp', None, 'seq'), may hold values from -0.15625 to 0.15625
- w_out: bfloat16 [16, 5120, 1280], P('exp', 'seq'), may hold values from -0.078125 to 0.078125
Outputs:
- mixed: bfloat16 [524288, 1280], P(('dp', 'seq', 'exp')), parts along dimension 0
The draws below stay inside these ranges and needn't reach their ends.
There are 2 independent parts, one for each index of `dp`. The reference program is written for one: setup_inputs(seed, part) draws one part's arguments, and reference() takes and returns one part's arrays. A program takes and returns all parts, laid end to end along the dimension named above; an argument that names none is the same for every part. Nothing has to cross between parts.
All inputs are finite; a program needn't handle non-finite values.
Results may differ from the reference program's by a relative error of at most 0.007.
Values may be sent and summed in bfloat16 or wider, within the bound.
No kernel may reach another device: no remote copies, remote signals or barrier semaphores. Data moves between devices by JAX's collectives and lax.ppermute only.
A program may use at most 64 MiB of HBM per device.

```python
import math
import jax
import jax.numpy as jnp
from jax import lax

D = 1280
FF = 5120
SLOTS_EXP = 16
EXPERTS = 16
SLOTS = 256
TOKENS = 262144


def draw_slot_keys(key, part):
    key = jax.random.fold_in(key, 5)
    values = jnp.clip(jax.random.normal(key, (D, SLOTS), jnp.float32), -6.0, 6.0) / math.sqrt(D)
    return values.astype(jnp.bfloat16)


def draw_tokens(key, part):
    key = jax.random.fold_in(key, 7)
    normal_part = jnp.clip(jax.random.normal(jax.random.fold_in(key, 1), (TOKENS, D), jnp.float32), -6.0, 6.0)
    scales = jnp.exp(jax.random.uniform(jax.random.fold_in(key, 2), (TOKENS, 1), jnp.float32, math.log(0.5), math.log(3.0)))
    values = normal_part * scales
    return values.astype(jnp.bfloat16)


def steps_of(rng, shape, pieces, least, largest):
    def one(position, shards_of):
        heights = jax.random.uniform(jax.random.fold_in(jax.random.fold_in(rng, 6), position), (shards_of,), jnp.float32, least / len(pieces), largest / len(pieces))
        return jnp.repeat(jnp.exp(heights), shape[position] // shards_of).reshape((-1,) + (1,) * (len(shape) - position - 1))

    level = one(*pieces[0])
    for cut in pieces[1:]:
        level = level * one(*cut)
    return level


def noise(own_key, extent, width, bound, split=(), held_as=jnp.bfloat16):
    entries = width * jax.random.normal(own_key, extent, jnp.float32)
    if split:
        entries = entries * steps_of(own_key, extent, split, -0.22, 0.18)
    return jnp.clip(entries, -bound, bound).astype(held_as)


def setup_inputs(seed: int = 0, part: int = 0) -> dict:
    seeds = jax.random.split(jax.random.key(seed), 5)
    own_keys = jax.random.split(jax.random.fold_in(seeds[4], part), 5)
    return {
        "tokens": draw_tokens(jax.random.fold_in(jax.random.fold_in(seeds[4], part), 71), part),
        "slot_keys": draw_slot_keys(jax.random.fold_in(seeds[4], 71), part),
        "w_in": noise(seeds[2], (EXPERTS, D, FF), D ** -0.5, 0.15625, ((0, 16), (2, 8))),
        "w_out": noise(seeds[3], (EXPERTS, FF, D), FF ** -0.5, 0.078125, ((0, 16), (1, 8))),
    }


def expert_rows(inputs):
    slot_block, first, second = inputs
    hidden = jax.nn.gelu(jnp.dot(slot_block, first, preferred_element_type=jnp.float32)).astype(jnp.bfloat16)
    return jnp.dot(hidden, second, preferred_element_type=jnp.float32).astype(jnp.bfloat16)


def reference(tokens, slot_keys, w_in, w_out):
    logits = jnp.dot(tokens, slot_keys, preferred_element_type=jnp.float32)
    slot_peak = jnp.max(logits, axis=0)
    spread = jnp.exp(logits - slot_peak[None, :])
    slot_total = jnp.sum(spread, axis=0)
    dispatch = spread.astype(jnp.bfloat16)
    weighted = jnp.dot(dispatch.T, tokens, preferred_element_type=jnp.float32)
    slot_in = (weighted / slot_total[:, None]).astype(jnp.bfloat16)
    slot_out = lax.map(expert_rows, (slot_in.reshape(EXPERTS, SLOTS_EXP, D), w_in, w_out))
    slot_out = slot_out.reshape(SLOTS, D)
    row_peak = jnp.max(logits, axis=1)
    row_exp = jnp.exp(logits - row_peak[:, None])
    combine = (row_exp / jnp.sum(row_exp, axis=1)[:, None]).astype(jnp.bfloat16)
    return jnp.dot(combine, slot_out, preferred_element_type=jnp.float32).astype(jnp.bfloat16)
```

```python
import jax
import jax.numpy as jnp
from jax import lax
from jax.sharding import PartitionSpec as P

F32 = jnp.float32
BF16 = jnp.bfloat16


def _core_perm():
    return [(s, s ^ 1) for s in range(8)]


def _x_perm(k):
    return [(s, ((s // 2 + k) % 4) * 2 + s % 2) for s in range(8)]


def _y_perm(k):
    return [(e, ((e // 4 + k) % 4) * 4 + e % 4) for e in range(16)]


def _z_perm(k):
    return [(e, (e // 4) * 4 + (e % 4 + k) % 4) for e in range(16)]


def _pieces(v, n):
    out = []
    for _ in range(n):
        p = lax.reduce_precision(v, 8, 7)
        out.append(p[:, None])
        v = v - p
    return out


def _pack16(sums, peak, total):
    rows = sums.shape[0]
    stats = _pieces(peak, 3) + _pieces(total, 3) + [jnp.zeros((rows, 122), F32)]
    return jnp.concatenate([sums] + stats, axis=1).astype(BF16)


def _unpack16(packed):
    n = packed.shape[1] - 128
    v = packed.astype(F32)
    return (
        v[:, :n],
        v[:, n] + v[:, n + 1] + v[:, n + 2],
        v[:, n + 3] + v[:, n + 4] + v[:, n + 5],
    )


def _pack32(sums, peak, total):
    rows = sums.shape[0]
    return jnp.concatenate(
        [sums, peak[:, None], total[:, None], jnp.zeros((rows, 126), F32)], axis=1
    )


def _unpack32(v):
    n = v.shape[1] - 128
    return v[:, :n], v[:, n], v[:, n + 1]


def _merge(parts):
    peak = parts[0][1]
    for _, p, _ in parts[1:]:
        peak = jnp.maximum(peak, p)
    sums, total = 0.0, 0.0
    for s, p, t in parts:
        a = jnp.exp(p - peak)
        sums = sums + s * a[:, None]
        total = total + t * a
    return sums, peak, total


def body(tokens, slot_keys, w_in, w_out):
    seq, exp = lax.axis_index("seq"), lax.axis_index("exp")
    core, y, z = seq % 2, exp // 4, exp % 4
    slots, width = slot_keys.shape[1], tokens.shape[1]
    half = width // 2

    logits = jnp.dot(tokens, slot_keys, preferred_element_type=F32)
    peak = jnp.max(logits, axis=0)
    spread = jnp.exp(logits - peak[None, :])
    total = jnp.sum(spread, axis=0)
    sums = lax.dot_general(
        spread.astype(BF16), tokens, (((0,), (0,)), ((), ())), preferred_element_type=F32
    )

    mine = lax.dynamic_slice_in_dim(sums, core * half, half, 1)
    other = lax.dynamic_slice_in_dim(sums, (1 - core) * half, half, 1)
    got = lax.ppermute(_pack16(other, peak, total), "seq", _core_perm())
    state = _merge([(mine, peak, total), _unpack16(got)])

    packed = _pack16(*state)
    rows = slots // 4
    got = [
        lax.ppermute(
            lax.dynamic_slice_in_dim(packed, ((y + k) % 4) * rows, rows, 0), "exp", _y_perm(k)
        )
        for k in range(1, 4)
    ]
    own = [lax.dynamic_slice_in_dim(v, y * rows, rows, 0) for v in state]
    state = _merge([tuple(own)] + [_unpack16(g) for g in got])

    packed = _pack32(*state)
    rows = rows // 4
    got = [
        lax.ppermute(
            lax.dynamic_slice_in_dim(packed, ((z + k) % 4) * rows, rows, 0), "exp", _z_perm(k)
        )
        for k in range(1, 4)
    ]
    own = lax.dynamic_slice_in_dim(packed, z * rows, rows, 0)
    state = _merge([_unpack32(g) for g in [own] + got])

    packed = _pack32(*state)
    got = [lax.ppermute(packed, "seq", _x_perm(k)) for k in range(1, 4)]
    sums, _, total = _merge([state] + [_unpack32(g) for g in got])
    slot_half = (sums / total[:, None]).astype(BF16)
    got = lax.ppermute(slot_half, "seq", _core_perm())
    slot_in = jnp.where(
        core == 0,
        jnp.concatenate([slot_half, got], axis=1),
        jnp.concatenate([got, slot_half], axis=1),
    )

    hidden = jax.nn.gelu(jnp.dot(slot_in, w_in[0], preferred_element_type=F32)).astype(BF16)
    partial = jnp.dot(hidden, w_out[0], preferred_element_type=F32)

    mine = lax.dynamic_slice_in_dim(partial, core * half, half, 1)
    other = lax.dynamic_slice_in_dim(partial, (1 - core) * half, half, 1)
    part = mine + lax.ppermute(other, "seq", _core_perm())
    whole = part + sum(lax.ppermute(part, "seq", _x_perm(k)) for k in range(1, 4))
    out = whole.astype(BF16)

    def spread_out(block, index, perm):
        rows = block.shape[0]
        res = jnp.zeros((4 * rows, block.shape[1]), block.dtype)
        got = [block] + [lax.ppermute(block, "exp", perm(k)) for k in range(1, 4)]
        for k, g in enumerate(got):
            res = lax.dynamic_update_slice_in_dim(res, g, ((index - k) % 4) * rows, 0)
        return res

    out = spread_out(out, z, _z_perm)
    out = spread_out(out, y, _y_perm)
    got = lax.ppermute(out, "seq", _core_perm())
    slot_out = jnp.where(
        core == 0,
        jnp.concatenate([out, got], axis=1),
        jnp.concatenate([got, out], axis=1),
    )

    row_peak = jnp.max(logits, axis=1)
    row_exp = jnp.exp(logits - row_peak[:, None])
    combine = (row_exp / jnp.sum(row_exp, axis=1)[:, None]).astype(BF16)
    return jnp.dot(combine, slot_out, preferred_element_type=F32).astype(BF16)


def solution(mesh):
    return jax.shard_map(
        body,
        mesh=mesh,
        in_specs=(P(("dp", "seq", "exp"), None), P(), P("exp", None, "seq"), P("exp", "seq", None)),
        out_specs=P(("dp", "seq", "exp"), None),
        check_vma=False,
    )
```

```python
import functools

import jax
import jax.numpy as jnp
from jax import lax
from jax.experimental import pallas as pl
from jax.experimental.pallas import tpu as pltpu
from jax.sharding import PartitionSpec as P

F32 = jnp.float32
BF16 = jnp.bfloat16
LANES = 128
VMEM = pl.BlockSpec(memory_space=pltpu.VMEM)
SMEM = pl.BlockSpec(memory_space=pltpu.SMEM)
ANY = pl.BlockSpec(memory_space=pl.ANY)


def _core_perm():
    return [(s, s ^ 1) for s in range(8)]


def _x_perm(k):
    return [(s, ((s // 2 + k) % 4) * 2 + s % 2) for s in range(8)]


def _y_perm(k):
    return [(e, ((e // 4 + k) % 4) * 4 + e % 4) for e in range(16)]


def _z_perm(k):
    return [(e, (e // 4) * 4 + (e % 4 + k) % 4) for e in range(16)]


def _call(kernel, name, out_shape, in_specs, scratch=(), out_specs=None, flops=0, bytes_accessed=0, **kw):
    many = isinstance(out_shape, list)
    if out_specs is None:
        out_specs = [VMEM] * len(out_shape) if many else VMEM
    return pl.pallas_call(
        kernel,
        in_specs=in_specs,
        out_specs=out_specs,
        out_shape=out_shape,
        scratch_shapes=list(scratch),
        compiler_params=pltpu.CompilerParams(vmem_limit_bytes=36 << 20),
        cost_estimate=pl.CostEstimate(flops=flops, bytes_accessed=bytes_accessed, transcendentals=0),
        name=name,
        **kw,
    )


def _stats(peak, total, n):
    lane = lax.broadcasted_iota(jnp.int32, (n, LANES), 1)
    st = jnp.zeros((n, LANES), F32)
    j = 0
    for v in (peak, total):
        for _ in range(3):
            p = v.astype(BF16).astype(F32)
            st = jnp.where(lane == j, p, st)
            v = v - p
            j += 1
    return st


def _read16(packed):
    n = packed.shape[1] - LANES
    v = packed.astype(F32)
    st = v[:, n:]
    return (
        v[:, :n],
        st[:, 0:1] + st[:, 1:2] + st[:, 2:3],
        st[:, 3:4] + st[:, 4:5] + st[:, 5:6],
    )


def _read32(v):
    n = v.shape[1] - LANES
    return v[:, :n], v[:, n : n + 1], v[:, n + 1 : n + 2]


def _pair(peak, total, n):
    lane = lax.broadcasted_iota(jnp.int32, (n, LANES), 1)
    return jnp.where(lane == 0, peak, jnp.where(lane == 1, total, 0.0))


def _merge(parts):
    peak = parts[0][1]
    for _, p, _ in parts[1:]:
        peak = jnp.maximum(peak, p)
    sums, total = None, None
    for s, p, t in parts:
        a = jnp.exp(p - peak)
        sums = s * a if sums is None else sums + s * a
        total = t * a if total is None else total + t * a
    return sums, peak, total


def _fold(v, op):
    out = v[:, :LANES]
    for j in range(1, v.shape[1] // LANES):
        out = op(out, v[:, j * LANES : (j + 1) * LANES])
    return out


def first_kernel(chunks, where, tok_hbm, keys_hbm, tok, logits, dispatch, packed, stat, keys, sem):
    tokens, width = tok.shape
    slots = logits.shape[0]
    half = width // 2
    step = tokens // chunks
    keys_copy = pltpu.make_async_copy(keys_hbm, keys, sem.at[chunks])
    keys_copy.start()
    copies = [
        pltpu.make_async_copy(
            tok_hbm.at[pl.ds(i * step, step)], tok.at[pl.ds(i * step, step)], sem.at[i]
        )
        for i in range(chunks)
    ]
    for c in copies:
        c.start()
    keys_copy.wait()
    keys_t = keys[...].T
    peak = None
    for i in range(chunks):
        copies[i].wait()
        part = lax.dot_general(
            keys_t,
            tok[i * step : (i + 1) * step, :],
            (((1,), (1,)), ((), ())),
            preferred_element_type=F32,
        )
        logits[:, i * step : (i + 1) * step] = part
        p = _fold(part, jnp.maximum)
        peak = p if peak is None else jnp.maximum(peak, p)
    peak = jnp.max(peak, axis=1, keepdims=True)
    total = None
    for i in range(chunks):
        e = jnp.exp(logits[:, i * step : (i + 1) * step] - peak)
        dispatch[:, i * step : (i + 1) * step] = e.astype(BF16)
        p = _fold(e, jnp.add)
        total = p if total is None else total + p
    total = jnp.sum(total, axis=1, keepdims=True)
    off = pl.multiple_of((1 - where[0]) * half, LANES)
    sums = jnp.dot(dispatch[...], tok[:, pl.ds(off, half)], preferred_element_type=F32)
    packed[:, :half] = sums.astype(BF16)
    packed[:, half:] = _stats(peak, total, slots).astype(BF16)
    stat[...] = _pair(peak, total, slots)


def own_kernel(where, tok, dispatch, stat, own):
    half = tok.shape[1] // 2
    off = pl.multiple_of(where[0] * half, LANES)
    own[:, :half] = jnp.dot(dispatch[...], tok[:, pl.ds(off, half)], preferred_element_type=F32)
    own[:, half:] = stat[...]


def combine_kernel(logits, combine):
    v = logits[...]
    e = jnp.exp(v - jnp.max(v, axis=0, keepdims=True))
    combine[...] = (e / jnp.sum(e, axis=0, keepdims=True)).astype(BF16).T


def core_merge_kernel(where, own, got, keep, send1, send2, send3):
    rows = keep.shape[0]
    half = own.shape[1] - LANES
    for k, ref in enumerate((keep, send1, send2, send3)):
        start = pl.multiple_of(lax.rem(where[1] + k, 4) * rows, rows)
        sums, peak, total = _merge(
            [_read32(own[pl.ds(start, rows), :]), _read16(got[pl.ds(start, rows), :])]
        )
        ref[:, :half] = sums.astype(ref.dtype)
        st = _pair(peak, total, rows) if k == 0 else _stats(peak, total, rows)
        ref[:, half:] = st.astype(ref.dtype)


def y_merge_kernel(where, own, got1, got2, got3, keep, send1, send2, send3):
    rows = keep.shape[0]
    half = own.shape[1] - LANES
    for k, ref in enumerate((keep, send1, send2, send3)):
        part = pl.ds(pl.multiple_of(lax.rem(where[2] + k, 4) * rows, rows), rows)
        sums, peak, total = _merge(
            [_read32(own[part, :])] + [_read16(g[part, :]) for g in (got1, got2, got3)]
        )
        ref[:, :half] = sums
        ref[:, half:] = _pair(peak, total, rows)


def z_merge_kernel(own, got1, got2, got3, out):
    half = own.shape[1] - LANES
    sums, peak, total = _merge([_read32(g[...]) for g in (own, got1, got2, got3)])
    out[:, :half] = sums
    out[:, half:] = _pair(peak, total, out.shape[0])


def x_merge_kernel(own, got1, got2, got3, out):
    sums, _, total = _merge([_read32(g[...]) for g in (own, got1, got2, got3)])
    out[...] = (sums / total).astype(BF16)


def mix_kernel(chunks, where, combine, own, other, out_hbm, slot_out, buf, sem):
    half = own.shape[1]
    step = combine.shape[0] // chunks
    slot_out[:, pl.ds(pl.multiple_of(where[0] * half, LANES), half)] = own[...]
    slot_out[:, pl.ds(pl.multiple_of((1 - where[0]) * half, LANES), half)] = other[...]
    copies = []
    depth = buf.shape[0]
    for i in range(chunks):
        if i >= depth:
            copies[i - depth].wait()
        buf[i % depth] = jnp.dot(
            combine[i * step : (i + 1) * step, :], slot_out[...], preferred_element_type=F32
        ).astype(BF16)
        c = pltpu.make_async_copy(
            buf.at[i % depth], out_hbm.at[pl.ds(i * step, step)], sem.at[i % depth]
        )
        c.start()
        copies.append(c)
    for c in copies[-depth:]:
        c.wait()


def body(tokens, slot_keys, w_in, w_out):
    seq, exp = lax.axis_index("seq"), lax.axis_index("exp")
    core, y, z = seq % 2, exp // 4, exp % 4
    where = jnp.stack([core, y, z]).astype(jnp.int32)
    count, width = tokens.shape
    slots = slot_keys.shape[1]
    half = width // 2
    packed_width = half + LANES
    chunks = 4

    tok, logits, dispatch, packed, stat = _call(
        functools.partial(first_kernel, chunks),
        "logits_and_sums",
        [
            pltpu.VMEM((count, width), BF16),
            pltpu.VMEM((slots, count), F32),
            pltpu.VMEM((slots, count), BF16),
            pltpu.VMEM((slots, packed_width), BF16),
            pltpu.VMEM((slots, LANES), F32),
        ],
        [SMEM, ANY, ANY],
        [pltpu.VMEM((width, slots), BF16), pltpu.SemaphoreType.DMA((chunks + 1,))],
        flops=3 * count * slots * width,
        bytes_accessed=2 * count * width,
    )(where, tokens, slot_keys)

    got = lax.ppermute(packed, "seq", _core_perm())
    own = _call(
        own_kernel,
        "own_sums",
        pltpu.VMEM((slots, packed_width), F32),
        [SMEM, VMEM, VMEM, VMEM],
        flops=count * slots * width,
    )(where, tok, dispatch, stat)
    combine = _call(
        combine_kernel,
        "combine",
        pltpu.VMEM((count, slots), BF16),
        [VMEM],
        flops=10 * count * slots,
    )(logits)

    rows = slots // 4
    own, *send = _call(
        core_merge_kernel,
        "core_merge",
        [pltpu.VMEM((rows, packed_width), F32)] + [pltpu.VMEM((rows, packed_width), BF16)] * 3,
        [SMEM, VMEM, VMEM],
    )(where, own, got)
    got = [lax.ppermute(v, "exp", _y_perm(k + 1)) for k, v in enumerate(send)]

    rows = rows // 4
    own, *send = _call(
        y_merge_kernel,
        "y_merge",
        [pltpu.VMEM((rows, packed_width), F32)] * 4,
        [SMEM] + [VMEM] * 4,
    )(where, own, *got)
    got = [lax.ppermute(v, "exp", _z_perm(k + 1)) for k, v in enumerate(send)]

    own = _call(
        z_merge_kernel, "z_merge", pltpu.VMEM((rows, packed_width), F32), [VMEM] * 4
    )(own, *got)
    got = [lax.ppermute(own, "seq", _x_perm(k)) for k in range(1, 4)]
    slot_half = _call(x_merge_kernel, "x_merge", pltpu.VMEM((rows, half), BF16), [VMEM] * 4)(
        own, *got
    )
    got = lax.ppermute(slot_half, "seq", _core_perm())
    slot_in = jnp.where(
        core == 0,
        jnp.concatenate([slot_half, got], axis=1),
        jnp.concatenate([got, slot_half], axis=1),
    )

    hidden = jax.nn.gelu(jnp.dot(slot_in, w_in[0], preferred_element_type=F32)).astype(BF16)
    partial = jnp.dot(hidden, w_out[0], preferred_element_type=F32)

    mine = lax.dynamic_slice_in_dim(partial, core * half, half, 1)
    other = lax.dynamic_slice_in_dim(partial, (1 - core) * half, half, 1)
    part = mine + lax.ppermute(other, "seq", _core_perm())
    whole = part + sum(lax.ppermute(part, "seq", _x_perm(k)) for k in range(1, 4))
    out = whole.astype(BF16)

    def gather(block, index, perm):
        n = block.shape[0]
        res = jnp.zeros((4 * n, block.shape[1]), block.dtype)
        blocks = [block] + [lax.ppermute(block, "exp", perm(k)) for k in range(1, 4)]
        for k, g in enumerate(blocks):
            res = lax.dynamic_update_slice_in_dim(res, g, ((index - k) % 4) * n, 0)
        return res

    out = gather(out, z, _z_perm)
    out = gather(out, y, _y_perm)
    other = lax.ppermute(out, "seq", _core_perm())

    steps = 8
    return _call(
        functools.partial(mix_kernel, steps),
        "mix",
        jax.ShapeDtypeStruct((count, width), BF16),
        [SMEM, VMEM, VMEM, VMEM],
        [
            pltpu.VMEM((slots, width), BF16),
            pltpu.VMEM((4, count // steps, width), BF16),
            pltpu.SemaphoreType.DMA((4,)),
        ],
        out_specs=ANY,
    )(where, combine, out, other)


def solution(mesh):
    return jax.shard_map(
        body,
        mesh=mesh,
        in_specs=(P(("dp", "seq", "exp"), None), P(), P("exp", None, "seq"), P("exp", "seq", None)),
        out_specs=P(("dp", "seq", "exp"), None),
        check_vma=False,
    )
```

```python
import functools

import jax
import jax.numpy as jnp
from jax import lax
from jax.experimental import pallas as pl
from jax.experimental.pallas import tpu as pltpu
from jax.sharding import PartitionSpec as P

F32 = jnp.float32
BF16 = jnp.bfloat16
LANES = 128
VMEM = pl.BlockSpec(memory_space=pltpu.VMEM)
SMEM = pl.BlockSpec(memory_space=pltpu.SMEM)
ANY = pl.BlockSpec(memory_space=pl.ANY)


def _core_perm():
    return [(s, s ^ 1) for s in range(8)]


def _x_perm(k):
    return [(s, ((s // 2 + k) % 4) * 2 + s % 2) for s in range(8)]


def _y_perm(k):
    return [(e, ((e // 4 + k) % 4) * 4 + e % 4) for e in range(16)]


def _z_perm(k):
    return [(e, (e // 4) * 4 + (e % 4 + k) % 4) for e in range(16)]


def _call(kernel, name, out_shape, in_specs, scratch=(), out_specs=None, vmem=6, flops=0, bytes_accessed=0, **kw):
    many = isinstance(out_shape, list)
    if out_specs is None:
        out_specs = [VMEM] * len(out_shape) if many else VMEM
    return pl.pallas_call(
        kernel,
        in_specs=in_specs,
        out_specs=out_specs,
        out_shape=out_shape,
        scratch_shapes=list(scratch),
        compiler_params=pltpu.CompilerParams(vmem_limit_bytes=vmem << 20),
        cost_estimate=pl.CostEstimate(flops=flops, bytes_accessed=bytes_accessed, transcendentals=0),
        name=name,
        **kw,
    )


def _lane(n):
    return lax.broadcasted_iota(jnp.int32, (n, LANES), 1)


def _wide(v):
    return jnp.broadcast_to(v, (v.shape[0], LANES))


def _pieces(peak, total):
    lane = _lane(peak.shape[0])
    st = jnp.zeros(peak.shape, F32)
    j = 0
    for v in (peak, total):
        for _ in range(3):
            p = v.astype(BF16).astype(F32)
            st = jnp.where(lane == j, p, st)
            v = v - p
            j += 1
    return st.astype(BF16)


def _unpieces(st):
    row = lax.broadcasted_iota(jnp.int32, (LANES, 2 * LANES), 0)
    column = lax.broadcasted_iota(jnp.int32, (LANES, 2 * LANES), 1)
    first = jnp.where(column < LANES, 0, 3)
    pick = jnp.where((row >= first) & (row < first + 3), 1.0, 0.0).astype(BF16)
    both = jnp.dot(st, pick, preferred_element_type=F32)
    return both[:, :LANES], both[:, LANES:]


def _pair(peak, total):
    lane = _lane(peak.shape[0])
    return jnp.where(lane == 0, peak, jnp.where(lane == 1, total, 0.0))


def _unpair(st):
    return _wide(st[:, 0:1]), _wide(st[:, 1:2])


def _times(v, scale):
    return jnp.concatenate(
        [v[:, j : j + LANES] * scale for j in range(0, v.shape[1], LANES)], axis=1
    )


def _merge(parts):
    peak = parts[0][1]
    for _, p, _ in parts[1:]:
        peak = jnp.maximum(peak, p)
    sums, total = None, None
    for s, p, t in parts:
        a = jnp.exp(p - peak)
        sums = _times(s, a) if sums is None else sums + _times(s, a)
        total = t * a if total is None else total + t * a
    return sums, peak, total


def _fold(v, op):
    out = v[:, :LANES]
    for j in range(1, v.shape[1] // LANES):
        out = op(out, v[:, j * LANES : (j + 1) * LANES])
    return out


def first_kernel(chunks, where, tok_hbm, keys_hbm, tok, logits, dispatch, packed, stat, keys, acc, sem):
    tokens, width = tok.shape
    half = width // 2
    step = tokens // chunks
    keys_copy = pltpu.make_async_copy(keys_hbm, keys, sem.at[chunks])
    keys_copy.start()
    copies = [
        pltpu.make_async_copy(
            tok_hbm.at[pl.ds(i * step, step)], tok.at[pl.ds(i * step, step)], sem.at[i]
        )
        for i in range(chunks)
    ]
    for c in copies:
        c.start()
    other = pl.multiple_of((1 - where[0]) * half, LANES)
    keys_copy.wait()
    keys_t = keys[...].T

    def weigh(i):
        return jnp.dot(
            dispatch[:, i * step : (i + 1) * step],
            tok[i * step : (i + 1) * step, pl.ds(other, half)],
            preferred_element_type=F32,
        )

    peaks, total = [], None
    for i in range(chunks):
        copies[i].wait()
        part = lax.dot_general(
            keys_t,
            tok[i * step : (i + 1) * step, :],
            (((1,), (1,)), ((), ())),
            preferred_element_type=F32,
        )
        logits[:, i * step : (i + 1) * step] = part
        peak = _wide(jnp.max(_fold(part, jnp.maximum), axis=1, keepdims=True))
        if i:
            peak = jnp.maximum(peak, peaks[-1])
        e = jnp.concatenate(
            [jnp.exp(part[:, j : j + LANES] - peak) for j in range(0, step, LANES)], axis=1
        )
        if i == 1:
            acc[...] = _times(weigh(0), jnp.exp(peaks[0] - peak))
        elif i > 1:
            acc[...] = _times(acc[...] + weigh(i - 1), jnp.exp(peaks[-1] - peak))
        dispatch[:, i * step : (i + 1) * step] = e.astype(BF16)
        add = _fold(e, jnp.add)
        total = add if i == 0 else total * jnp.exp(peaks[-1] - peak) + add
        peaks.append(peak)
    total = _wide(jnp.sum(total, axis=1, keepdims=True))
    sums = acc[...] + weigh(chunks - 1)
    packed[:, :half] = sums.astype(BF16)
    packed[:, half:] = _pieces(peak, total)
    stat[:, :LANES] = peak
    stat[:, LANES : 2 * LANES] = total
    for i in range(chunks):
        stat[:, (2 + i) * LANES : (3 + i) * LANES] = jnp.exp(peaks[i] - peak)


def own_kernel(chunks, where, tok, dispatch, stat, own):
    half = tok.shape[1] // 2
    step = tok.shape[0] // chunks
    off = pl.multiple_of(where[0] * half, LANES)
    sums = None
    for i in range(chunks):
        part = _times(
            jnp.dot(
                dispatch[:, i * step : (i + 1) * step],
                tok[i * step : (i + 1) * step, pl.ds(off, half)],
                preferred_element_type=F32,
            ),
            stat[:, (2 + i) * LANES : (3 + i) * LANES],
        )
        sums = part if sums is None else sums + part
    own[...] = sums


def combine_kernel(after, logits, w_in_hbm, w_out_hbm, combine, w_in, w_out, sem):
    copies = [
        pltpu.make_async_copy(w_in_hbm, w_in, sem.at[0]),
        pltpu.make_async_copy(w_out_hbm, w_out, sem.at[1]),
    ]
    for c in copies:
        c.start()
    v = logits[...]
    e = jnp.exp(v - jnp.max(v, axis=0, keepdims=True))
    combine[...] = (e / jnp.sum(e, axis=0, keepdims=True)).astype(BF16).T
    for c in copies:
        c.wait()


def expert_kernel(where, slot_own, slot_other, w_in, w_out, own, send):
    half = slot_own.shape[1]
    mine = pl.multiple_of(where[0] * half, LANES)
    other = pl.multiple_of((1 - where[0]) * half, LANES)
    hidden = jnp.dot(slot_own[...], w_in[pl.ds(mine, half), :], preferred_element_type=F32)
    hidden += jnp.dot(slot_other[...], w_in[pl.ds(other, half), :], preferred_element_type=F32)
    hidden = jax.nn.gelu(hidden).astype(BF16)
    send[...] = jnp.dot(hidden, w_out[:, pl.ds(other, half)], preferred_element_type=F32)
    own[...] = jnp.dot(hidden, w_out[:, pl.ds(mine, half)], preferred_element_type=F32)


def core_merge_kernel(where, own, stat, got, keep, keep_stat, send1, send2, send3):
    rows, half = keep.shape
    for k, ref in enumerate((keep, send1, send2, send3)):
        part = pl.ds(pl.multiple_of(lax.rem(where[1] + k, 4) * rows, rows), rows)
        sums, peak, total = _merge(
            [
                (own[part, :], stat[part, :LANES], stat[part, LANES : 2 * LANES]),
                (got[part, :half].astype(F32), *_unpieces(got[part, half:])),
            ]
        )
        ref[:, :half] = sums.astype(ref.dtype)
        if k == 0:
            keep_stat[:, :LANES] = peak
            keep_stat[:, LANES:] = total
        else:
            ref[:, half:] = _pieces(peak, total)


def y_merge_kernel(where, after, own, stat, got1, got2, got3, keep, send1, send2, send3):
    rows, half = keep.shape[0], own.shape[1]
    for k, ref in enumerate((keep, send1, send2, send3)):
        part = pl.ds(pl.multiple_of(lax.rem(where[2] + k, 4) * rows, rows), rows)
        sums, peak, total = _merge(
            [(own[part, :], stat[part, :LANES], stat[part, LANES:])]
            + [
                (g[part, :half].astype(F32), *_unpieces(g[part, half:]))
                for g in (got1, got2, got3)
            ]
        )
        ref[:, :half] = sums
        ref[:, half:] = _pair(peak, total)


def z_merge_kernel(own, got1, got2, got3, out):
    half = own.shape[1] - LANES
    sums, peak, total = _merge(
        [(g[:, :half], *_unpair(g[:, half:])) for g in (own, got1, got2, got3)]
    )
    out[:, :half] = sums
    out[:, half:] = _pair(peak, total)


def x_merge_kernel(own, got1, got2, got3, out):
    half = own.shape[1] - LANES
    sums, _, total = _merge(
        [(g[:, :half], *_unpair(g[:, half:])) for g in (own, got1, got2, got3)]
    )
    out[...] = (sums / _wide_as(total, half)).astype(BF16)


def _wide_as(v, width):
    return jnp.concatenate([v] * (width // LANES), axis=1)


def mix_kernel(chunks, own, where, combine, slot_out, *refs):
    out_hbm, buf, sem = refs[-3:]
    half = slot_out.shape[1]
    step = combine.shape[0] // chunks
    column = pl.multiple_of((where[0] if own else 1 - where[0]) * half, LANES)
    copies = []
    for i in range(chunks):
        buf[i] = jnp.dot(
            combine[i * step : (i + 1) * step, :], slot_out[...], preferred_element_type=F32
        ).astype(BF16)
        c = pltpu.make_async_copy(
            buf.at[i], out_hbm.at[pl.ds(i * step, step), pl.ds(column, half)], sem.at[i]
        )
        c.start()
        copies.append(c)
    for c in copies:
        c.wait()


def body(tokens, slot_keys, w_in, w_out):
    seq, exp = lax.axis_index("seq"), lax.axis_index("exp")
    y, z = exp // 4, exp % 4
    where = jnp.stack([seq % 2, y, z]).astype(jnp.int32)

    tok, logits, dispatch, packed, stat = first(where, tokens, slot_keys)
    got = lax.ppermute(packed, "seq", _core_perm())
    own = own_sums(where, tok, dispatch, stat)

    own, stat, *send = core_merge(where, own, stat, got)
    got = [lax.ppermute(v, "exp", _y_perm(k + 1)) for k, v in enumerate(send)]
    combine, w_in, w_out = combine_weights(own, logits, w_in[0], w_out[0])
    own, *send = y_merge(where, combine, own, stat, *got)
    got = [lax.ppermute(v, "exp", _z_perm(k + 1)) for k, v in enumerate(send)]
    own = z_merge(own, *got)
    got = [lax.ppermute(own, "seq", _x_perm(k)) for k in range(1, 4)]
    slot_half = x_merge(own, *got)
    got = lax.ppermute(slot_half, "seq", _core_perm())
    mine, other = expert(where, slot_half, got, w_in, w_out)
    part = mine + lax.ppermute(other, "seq", _core_perm())
    whole = part + sum(lax.ppermute(part, "seq", _x_perm(k)) for k in range(1, 4))
    out = whole.astype(BF16)

    def gather(block, index, perm):
        n = block.shape[0]
        res = jnp.zeros((4 * n, block.shape[1]), block.dtype)
        blocks = [block] + [lax.ppermute(block, "exp", perm(k)) for k in range(1, 4)]
        for k, g in enumerate(blocks):
            res = lax.dynamic_update_slice_in_dim(res, g, ((index - k) % 4) * n, 0)
        return res

    out = gather(out, z, _z_perm)
    out = gather(out, y, _y_perm)
    other = lax.ppermute(out, "seq", _core_perm())
    mixed = mix(where, combine, out)
    return mix(where, combine, other, mixed)


CHUNKS = 4


def first(where, tokens, slot_keys):
    count, width = tokens.shape
    slots = slot_keys.shape[1]
    half = width // 2
    return _call(
        functools.partial(first_kernel, CHUNKS),
        "logits_and_sums",
        [
            pltpu.VMEM((count, width), BF16),
            pltpu.VMEM((slots, count), F32),
            pltpu.VMEM((slots, count), BF16),
            pltpu.VMEM((slots, half + LANES), BF16),
            pltpu.VMEM((slots, (2 + CHUNKS) * LANES), F32),
        ],
        [SMEM, ANY, ANY],
        [
            pltpu.VMEM((width, slots), BF16),
            pltpu.VMEM((slots, half), F32),
            pltpu.SemaphoreType.DMA((CHUNKS + 1,)),
        ],
        vmem=16,
        flops=3 * count * slots * width,
        bytes_accessed=2 * count * width,
    )(where, *(pltpu.with_memory_space_constraint(v, pltpu.HBM) for v in (tokens, slot_keys)))


def own_sums(where, tok, dispatch, stat):
    return _call(
        functools.partial(own_kernel, CHUNKS),
        "own_sums",
        pltpu.VMEM((stat.shape[0], tok.shape[1] // 2), F32),
        [SMEM, VMEM, VMEM, VMEM],
        vmem=12,
        flops=dispatch.size * tok.shape[1],
    )(where, tok, dispatch, stat)


def combine_weights(after, logits, w_in, w_out):
    slots, count = logits.shape
    return _call(
        combine_kernel,
        "combine",
        [
            pltpu.VMEM((count, slots), BF16),
            pltpu.VMEM(w_in.shape, BF16),
            pltpu.VMEM(w_out.shape, BF16),
        ],
        [ANY, VMEM, ANY, ANY],
        [pltpu.SemaphoreType.DMA((2,))],
        vmem=12,
        flops=10 * count * slots,
        bytes_accessed=4 * w_in.size,
    )(after, logits, *(pltpu.with_memory_space_constraint(v, pltpu.HBM) for v in (w_in, w_out)))


def expert(where, slot_own, slot_other, w_in, w_out):
    return _call(
        expert_kernel,
        "expert",
        [pltpu.VMEM(slot_own.shape, F32)] * 2,
        [SMEM] + [VMEM] * 4,
        flops=4 * slot_own.shape[0] * w_in.size,
    )(where, slot_own, slot_other, w_in, w_out)


def core_merge(where, own, stat, got):
    rows, half = own.shape[0] // 4, own.shape[1]
    return _call(
        core_merge_kernel,
        "core_merge",
        [pltpu.VMEM((rows, half), F32), pltpu.VMEM((rows, 2 * LANES), F32)]
        + [pltpu.VMEM((rows, half + LANES), BF16)] * 3,
        [SMEM] + [VMEM] * 3,
    )(where, own, stat, got)


def y_merge(where, after, own, stat, *got):
    rows, half = own.shape[0] // 4, own.shape[1]
    return _call(
        y_merge_kernel,
        "y_merge",
        [pltpu.VMEM((rows, half + LANES), F32)] * 4,
        [SMEM, ANY] + [VMEM] * 5,
    )(where, after, own, stat, *got)


def z_merge(own, *got):
    return _call(z_merge_kernel, "z_merge", pltpu.VMEM(own.shape, F32), [VMEM] * 4)(own, *got)


def x_merge(own, *got):
    out = pltpu.VMEM((own.shape[0], own.shape[1] - LANES), BF16)
    return _call(x_merge_kernel, "x_merge", out, [VMEM] * 4)(own, *got)


def mix(where, combine, slot_out, *mixed):
    count, slots = combine.shape
    half = slot_out.shape[1]
    steps = 8
    return _call(
        functools.partial(mix_kernel, steps, not mixed),
        "mix",
        jax.ShapeDtypeStruct((count, 2 * half), BF16),
        [SMEM, VMEM, VMEM] + [ANY] * len(mixed),
        [pltpu.VMEM((steps, count // steps, half), BF16), pltpu.SemaphoreType.DMA((steps,))],
        out_specs=ANY,
        vmem=12,
        flops=2 * count * slots * half,
        bytes_accessed=2 * count * half,
        input_output_aliases={3: 0} if mixed else {},
    )(where, combine, slot_out, *mixed)


def solution(mesh):
    return jax.shard_map(
        body,
        mesh=mesh,
        in_specs=(P(("dp", "seq", "exp"), None), P(), P("exp", None, "seq"), P("exp", "seq", None)),
        out_specs=P(("dp", "seq", "exp"), None),
        check_vma=False,
    )
```

```python
import functools

import jax
import jax.numpy as jnp
from jax import lax
from jax.experimental import pallas as pl
from jax.experimental.pallas import tpu as pltpu
from jax.sharding import PartitionSpec as P

F32 = jnp.float32
BF16 = jnp.bfloat16
LANES = 128
VMEM = pl.BlockSpec(memory_space=pltpu.VMEM)
ANY = pl.BlockSpec(memory_space=pl.ANY)


def _core():
    return lax.rem(lax.axis_index("seq"), 2)


def _y():
    return lax.div(lax.axis_index("exp"), 4)


def _z():
    return lax.rem(lax.axis_index("exp"), 4)


def _core_perm():
    return [(s, s ^ 1) for s in range(8)]


def _x_perm(k):
    return [(s, ((s // 2 + k) % 4) * 2 + s % 2) for s in range(8)]


def _y_perm(k):
    return [(e, ((e // 4 + k) % 4) * 4 + e % 4) for e in range(16)]


def _z_perm(k):
    return [(e, (e // 4) * 4 + (e % 4 + k) % 4) for e in range(16)]


def _call(kernel, name, out_shape, in_specs, scratch=(), out_specs=None, vmem=6, flops=0, bytes_accessed=0, **kw):
    many = isinstance(out_shape, list)
    if out_specs is None:
        out_specs = [VMEM] * len(out_shape) if many else VMEM
    return pl.pallas_call(
        kernel,
        in_specs=in_specs,
        out_specs=out_specs,
        out_shape=out_shape,
        scratch_shapes=list(scratch),
        compiler_params=pltpu.CompilerParams(vmem_limit_bytes=vmem << 20),
        cost_estimate=pl.CostEstimate(flops=flops, bytes_accessed=bytes_accessed, transcendentals=0),
        name=name,
        **kw,
    )


def _lane(n):
    return lax.broadcasted_iota(jnp.int32, (n, LANES), 1)


def _wide(v):
    return jnp.broadcast_to(v, (v.shape[0], LANES))


def _pieces(peak, total):
    lane = _lane(peak.shape[0])
    st = jnp.zeros(peak.shape, F32)
    j = 0
    for v in (peak, total):
        for _ in range(3):
            p = v.astype(BF16).astype(F32)
            st = jnp.where(lane == j, p, st)
            v = v - p
            j += 1
    return st.astype(BF16)


def _unpieces(st):
    row = lax.broadcasted_iota(jnp.int32, (LANES, 2 * LANES), 0)
    column = lax.broadcasted_iota(jnp.int32, (LANES, 2 * LANES), 1)
    first = jnp.where(column < LANES, 0, 3)
    pick = jnp.where((row >= first) & (row < first + 3), 1.0, 0.0).astype(BF16)
    both = jnp.dot(st, pick, preferred_element_type=F32)
    return both[:, :LANES], both[:, LANES:]


def _pair(peak, total):
    lane = _lane(peak.shape[0])
    return jnp.where(lane == 0, peak, jnp.where(lane == 1, total, 0.0))


def _unpair(st):
    return _wide(st[:, 0:1]), _wide(st[:, 1:2])


def _times(v, scale):
    return jnp.concatenate(
        [v[:, j : j + LANES] * scale for j in range(0, v.shape[1], LANES)], axis=1
    )


def _merge(parts):
    peak = parts[0][1]
    for _, p, _ in parts[1:]:
        peak = jnp.maximum(peak, p)
    sums, total = None, None
    for s, p, t in parts:
        a = jnp.exp(p - peak)
        sums = _times(s, a) if sums is None else sums + _times(s, a)
        total = t * a if total is None else total + t * a
    return sums, peak, total


def _fold(v, op):
    out = v[:, :LANES]
    for j in range(1, v.shape[1] // LANES):
        out = op(out, v[:, j * LANES : (j + 1) * LANES])
    return out


def first_kernel(chunks, tok_hbm, keys_hbm, tok, logits, dispatch, packed, stat, keys, acc, sem):
    tokens, width = tok.shape
    half = width // 2
    step = tokens // chunks
    keys_copy = pltpu.make_async_copy(keys_hbm, keys, sem.at[chunks])
    keys_copy.start()
    copies = [
        pltpu.make_async_copy(
            tok_hbm.at[pl.ds(i * step, step)], tok.at[pl.ds(i * step, step)], sem.at[i]
        )
        for i in range(chunks)
    ]
    for c in copies:
        c.start()
    other = pl.multiple_of((1 - _core()) * half, LANES)
    keys_copy.wait()
    keys_t = keys[...].T

    def weigh(i):
        return jnp.dot(
            dispatch[:, i * step : (i + 1) * step],
            tok[i * step : (i + 1) * step, pl.ds(other, half)],
            preferred_element_type=F32,
        )

    peaks, total = [], None
    for i in range(chunks):
        copies[i].wait()
        part = lax.dot_general(
            keys_t,
            tok[i * step : (i + 1) * step, :],
            (((1,), (1,)), ((), ())),
            preferred_element_type=F32,
        )
        logits[:, i * step : (i + 1) * step] = part
        peak = _wide(jnp.max(_fold(part, jnp.maximum), axis=1, keepdims=True))
        if i:
            peak = jnp.maximum(peak, peaks[-1])
        e = jnp.concatenate(
            [jnp.exp(part[:, j : j + LANES] - peak) for j in range(0, step, LANES)], axis=1
        )
        if i == 1:
            acc[...] = _times(weigh(0), jnp.exp(peaks[0] - peak))
        elif i > 1:
            acc[...] = _times(acc[...] + weigh(i - 1), jnp.exp(peaks[-1] - peak))
        dispatch[:, i * step : (i + 1) * step] = e.astype(BF16)
        add = _fold(e, jnp.add)
        total = add if i == 0 else total * jnp.exp(peaks[-1] - peak) + add
        peaks.append(peak)
    total = _wide(jnp.sum(total, axis=1, keepdims=True))
    sums = acc[...] + weigh(chunks - 1)
    packed[:, :half] = sums.astype(BF16)
    packed[:, half:] = _pieces(peak, total)
    stat[:, :LANES] = peak
    stat[:, LANES : 2 * LANES] = total
    for i in range(chunks):
        stat[:, (2 + i) * LANES : (3 + i) * LANES] = jnp.exp(peaks[i] - peak)


def own_kernel(chunks, tok, dispatch, stat, own):
    half = tok.shape[1] // 2
    step = tok.shape[0] // chunks
    off = pl.multiple_of(_core() * half, LANES)
    sums = None
    for i in range(chunks):
        part = _times(
            jnp.dot(
                dispatch[:, i * step : (i + 1) * step],
                tok[i * step : (i + 1) * step, pl.ds(off, half)],
                preferred_element_type=F32,
            ),
            stat[:, (2 + i) * LANES : (3 + i) * LANES],
        )
        sums = part if sums is None else sums + part
    own[...] = sums


def combine_kernel(after, logits, w_in_hbm, w_out_hbm, combine, w_in, w_out, sem):
    copies = [
        pltpu.make_async_copy(w_in_hbm, w_in, sem.at[0]),
        pltpu.make_async_copy(w_out_hbm, w_out, sem.at[1]),
    ]
    for c in copies:
        c.start()
    v = logits[...]
    e = jnp.exp(v - jnp.max(v, axis=0, keepdims=True))
    combine[...] = (e / jnp.sum(e, axis=0, keepdims=True)).astype(BF16).T
    for c in copies:
        c.wait()


def expert_kernel(slot_own, slot_other, w_in, w_out, own, send):
    half = slot_own.shape[1]
    mine = pl.multiple_of(_core() * half, LANES)
    other = pl.multiple_of((1 - _core()) * half, LANES)
    hidden = jnp.dot(slot_own[...], w_in[pl.ds(mine, half), :], preferred_element_type=F32)
    hidden += jnp.dot(slot_other[...], w_in[pl.ds(other, half), :], preferred_element_type=F32)
    hidden = jax.nn.gelu(hidden).astype(BF16)
    send[...] = jnp.dot(hidden, w_out[:, pl.ds(other, half)], preferred_element_type=F32)
    own[...] = jnp.dot(hidden, w_out[:, pl.ds(mine, half)], preferred_element_type=F32)


def core_merge_kernel(own, stat, got, keep, keep_stat, send1, send2, send3):
    rows, half = keep.shape
    for k, ref in enumerate((keep, send1, send2, send3)):
        part = pl.ds(pl.multiple_of(lax.rem(_y() + k, 4) * rows, rows), rows)
        sums, peak, total = _merge(
            [
                (own[part, :], stat[part, :LANES], stat[part, LANES : 2 * LANES]),
                (got[part, :half].astype(F32), *_unpieces(got[part, half:])),
            ]
        )
        ref[:, :half] = sums.astype(ref.dtype)
        if k == 0:
            keep_stat[:, :LANES] = peak
            keep_stat[:, LANES:] = total
        else:
            ref[:, half:] = _pieces(peak, total)


def y_merge_kernel(after, own, stat, got1, got2, got3, keep, send1, send2, send3):
    rows, half = keep.shape[0], own.shape[1]
    for k, ref in enumerate((keep, send1, send2, send3)):
        part = pl.ds(pl.multiple_of(lax.rem(_z() + k, 4) * rows, rows), rows)
        sums, peak, total = _merge(
            [(own[part, :], stat[part, :LANES], stat[part, LANES:])]
            + [
                (g[part, :half].astype(F32), *_unpieces(g[part, half:]))
                for g in (got1, got2, got3)
            ]
        )
        ref[:, :half] = sums
        ref[:, half:] = _pair(peak, total)


def z_merge_kernel(own, got1, got2, got3, out):
    half = own.shape[1] - LANES
    sums, peak, total = _merge(
        [(g[:, :half], *_unpair(g[:, half:])) for g in (own, got1, got2, got3)]
    )
    out[:, :half] = sums
    out[:, half:] = _pair(peak, total)


def x_merge_kernel(own, got1, got2, got3, out):
    half = own.shape[1] - LANES
    sums, _, total = _merge(
        [(g[:, :half], *_unpair(g[:, half:])) for g in (own, got1, got2, got3)]
    )
    out[...] = (sums / _wide_as(total, half)).astype(BF16)


def _wide_as(v, width):
    return jnp.concatenate([v] * (width // LANES), axis=1)


def mix_kernel(chunks, own, combine, slot_out, *refs):
    out_hbm, buf, sem = refs[-3:]
    half = slot_out.shape[1]
    step = combine.shape[0] // chunks
    column = pl.multiple_of((_core() if own else 1 - _core()) * half, LANES)
    copies = []
    for i in range(chunks):
        buf[i] = jnp.dot(
            combine[i * step : (i + 1) * step, :], slot_out[...], preferred_element_type=F32
        ).astype(BF16)
        c = pltpu.make_async_copy(
            buf.at[i], out_hbm.at[pl.ds(i * step, step), pl.ds(column, half)], sem.at[i]
        )
        c.start()
        copies.append(c)
    for c in copies:
        c.wait()


def body(tokens, slot_keys, w_in, w_out):
    y, z = _y(), _z()

    tok, logits, dispatch, packed, stat = first(tokens, slot_keys)
    got = lax.ppermute(packed, "seq", _core_perm())
    own = own_sums(tok, dispatch, stat)

    own, stat, *send = core_merge(own, stat, got)
    got = [lax.ppermute(v, "exp", _y_perm(k + 1)) for k, v in enumerate(send)]
    combine, w_in, w_out = combine_weights(own, logits, w_in[0], w_out[0])
    own, *send = y_merge(combine, own, stat, *got)
    got = [lax.ppermute(v, "exp", _z_perm(k + 1)) for k, v in enumerate(send)]
    own = z_merge(own, *got)
    got = [lax.ppermute(own, "seq", _x_perm(k)) for k in range(1, 4)]
    slot_half = x_merge(own, *got)
    got = lax.ppermute(slot_half, "seq", _core_perm())
    mine, other = expert(slot_half, got, w_in, w_out)
    part = mine + lax.ppermute(other, "seq", _core_perm())
    whole = part + sum(lax.ppermute(part, "seq", _x_perm(k)) for k in range(1, 4))
    out = whole.astype(BF16)

    def gather(block, index, perm):
        n = block.shape[0]
        res = jnp.zeros((4 * n, block.shape[1]), block.dtype)
        blocks = [block] + [lax.ppermute(block, "exp", perm(k)) for k in range(1, 4)]
        for k, g in enumerate(blocks):
            res = lax.dynamic_update_slice_in_dim(res, g, ((index - k) % 4) * n, 0)
        return res

    out = gather(out, z, _z_perm)
    out = gather(out, y, _y_perm)
    other = lax.ppermute(out, "seq", _core_perm())
    mixed = mix(combine, out)
    return mix(combine, other, mixed)


CHUNKS = 4


def first(tokens, slot_keys):
    count, width = tokens.shape
    slots = slot_keys.shape[1]
    half = width // 2
    return _call(
        functools.partial(first_kernel, CHUNKS),
        "logits_and_sums",
        [
            pltpu.VMEM((count, width), BF16),
            pltpu.VMEM((slots, count), F32),
            pltpu.VMEM((slots, count), BF16),
            pltpu.VMEM((slots, half + LANES), BF16),
            pltpu.VMEM((slots, (2 + CHUNKS) * LANES), F32),
        ],
        [ANY, ANY],
        [
            pltpu.VMEM((width, slots), BF16),
            pltpu.VMEM((slots, half), F32),
            pltpu.SemaphoreType.DMA((CHUNKS + 1,)),
        ],
        vmem=16,
        flops=3 * count * slots * width,
        bytes_accessed=2 * count * width,
    )(*(pltpu.with_memory_space_constraint(v, pltpu.HBM) for v in (tokens, slot_keys)))


def own_sums(tok, dispatch, stat):
    return _call(
        functools.partial(own_kernel, CHUNKS),
        "own_sums",
        pltpu.VMEM((stat.shape[0], tok.shape[1] // 2), F32),
        [VMEM, VMEM, VMEM],
        vmem=12,
        flops=dispatch.size * tok.shape[1],
    )(tok, dispatch, stat)


def combine_weights(after, logits, w_in, w_out):
    slots, count = logits.shape
    return _call(
        combine_kernel,
        "combine",
        [
            pltpu.VMEM((count, slots), BF16),
            pltpu.VMEM(w_in.shape, BF16),
            pltpu.VMEM(w_out.shape, BF16),
        ],
        [ANY, VMEM, ANY, ANY],
        [pltpu.SemaphoreType.DMA((2,))],
        vmem=12,
        flops=10 * count * slots,
        bytes_accessed=4 * w_in.size,
    )(after, logits, *(pltpu.with_memory_space_constraint(v, pltpu.HBM) for v in (w_in, w_out)))


def expert(slot_own, slot_other, w_in, w_out):
    return _call(
        expert_kernel,
        "expert",
        [pltpu.VMEM(slot_own.shape, F32)] * 2,
        [VMEM] * 4,
        flops=4 * slot_own.shape[0] * w_in.size,
    )(slot_own, slot_other, w_in, w_out)


def core_merge(own, stat, got):
    rows, half = own.shape[0] // 4, own.shape[1]
    return _call(
        core_merge_kernel,
        "core_merge",
        [pltpu.VMEM((rows, half), F32), pltpu.VMEM((rows, 2 * LANES), F32)]
        + [pltpu.VMEM((rows, half + LANES), BF16)] * 3,
        [VMEM] * 3,
    )(own, stat, got)


def y_merge(after, own, stat, *got):
    rows, half = own.shape[0] // 4, own.shape[1]
    return _call(
        y_merge_kernel,
        "y_merge",
        [pltpu.VMEM((rows, half + LANES), F32)] * 4,
        [ANY] + [VMEM] * 5,
    )(after, own, stat, *got)


def z_merge(own, *got):
    return _call(z_merge_kernel, "z_merge", pltpu.VMEM(own.shape, F32), [VMEM] * 4)(own, *got)


def x_merge(own, *got):
    out = pltpu.VMEM((own.shape[0], own.shape[1] - LANES), BF16)
    return _call(x_merge_kernel, "x_merge", out, [VMEM] * 4)(own, *got)


def mix(combine, slot_out, *mixed):
    count, slots = combine.shape
    half = slot_out.shape[1]
    steps = 8
    return _call(
        functools.partial(mix_kernel, steps, not mixed),
        "mix",
        jax.ShapeDtypeStruct((count, 2 * half), BF16),
        [VMEM, VMEM] + [ANY] * len(mixed),
        [pltpu.VMEM((steps, count // steps, half), BF16), pltpu.SemaphoreType.DMA((steps,))],
        out_specs=ANY,
        vmem=12,
        flops=2 * count * slots * half,
        bytes_accessed=2 * count * half,
        input_output_aliases={2: 0} if mixed else {},
    )(combine, slot_out, *mixed)


def solution(mesh):
    return jax.shard_map(
        body,
        mesh=mesh,
        in_specs=(P(("dp", "seq", "exp"), None), P(), P("exp", None, "seq"), P("exp", "seq", None)),
        out_specs=P(("dp", "seq", "exp"), None),
        check_vma=False,
    )
```

```python
import functools

import jax
import jax.numpy as jnp
from jax import lax
from jax.experimental import pallas as pl
from jax.experimental.pallas import tpu as pltpu
from jax.sharding import PartitionSpec as P

F32 = jnp.float32
BF16 = jnp.bfloat16
LANES = 128
VMEM = pl.BlockSpec(memory_space=pltpu.VMEM)
ANY = pl.BlockSpec(memory_space=pl.ANY)


def _core():
    seq = lax.axis_index("seq")
    return lax.rem(seq + lax.div(seq, 2) + _y(), 2)


def _y():
    return lax.div(lax.axis_index("exp"), 4)


def _z():
    return lax.rem(lax.axis_index("exp"), 4)


def _core_perm():
    return [(s, s ^ 1) for s in range(8)]


def _x_perm(k):
    return [(s, ((s // 2 + k) % 4) * 2 + (s + k) % 2) for s in range(8)]


def _y_perm(k):
    return [
        (s * 16 + e, (s ^ (k & 1)) * 16 + ((e // 4 + k) % 4) * 4 + e % 4)
        for s in range(8)
        for e in range(16)
    ]


def _z_perm(k):
    return [(e, (e // 4) * 4 + (e % 4 + k) % 4) for e in range(16)]


def _call(kernel, name, out_shape, in_specs, scratch=(), out_specs=None, vmem=6, flops=0, bytes_accessed=0, **kw):
    many = isinstance(out_shape, list)
    if out_specs is None:
        out_specs = [VMEM] * len(out_shape) if many else VMEM
    return pl.pallas_call(
        kernel,
        in_specs=in_specs,
        out_specs=out_specs,
        out_shape=out_shape,
        scratch_shapes=list(scratch),
        compiler_params=pltpu.CompilerParams(vmem_limit_bytes=vmem << 20),
        cost_estimate=pl.CostEstimate(flops=flops, bytes_accessed=bytes_accessed, transcendentals=0),
        name=name,
        **kw,
    )


def _lane(n):
    return lax.broadcasted_iota(jnp.int32, (n, LANES), 1)


def _wide(v):
    return jnp.broadcast_to(v, (v.shape[0], LANES))


def _pieces(peak, total):
    lane = _lane(peak.shape[0])
    st = jnp.zeros(peak.shape, F32)
    j = 0
    for v in (peak, total):
        for _ in range(3):
            p = v.astype(BF16).astype(F32)
            st = jnp.where(lane == j, p, st)
            v = v - p
            j += 1
    return st.astype(BF16)


def _unpieces(st):
    row = lax.broadcasted_iota(jnp.int32, (LANES, 2 * LANES), 0)
    column = lax.broadcasted_iota(jnp.int32, (LANES, 2 * LANES), 1)
    first = jnp.where(column < LANES, 0, 3)
    pick = jnp.where((row >= first) & (row < first + 3), 1.0, 0.0).astype(BF16)
    both = jnp.dot(st, pick, preferred_element_type=F32)
    return both[:, :LANES], both[:, LANES:]


def _pair(peak, total):
    lane = _lane(peak.shape[0])
    return jnp.where(lane == 0, peak, jnp.where(lane == 1, total, 0.0))


def _unpair(st):
    return _wide(st[:, 0:1]), _wide(st[:, 1:2])


def _times(v, scale):
    return jnp.concatenate(
        [v[:, j : j + LANES] * scale for j in range(0, v.shape[1], LANES)], axis=1
    )


def _merge(parts):
    peak = parts[0][1]
    for _, p, _ in parts[1:]:
        peak = jnp.maximum(peak, p)
    sums, total = None, None
    for s, p, t in parts:
        a = jnp.exp(p - peak)
        sums = _times(s, a) if sums is None else sums + _times(s, a)
        total = t * a if total is None else total + t * a
    return sums, peak, total


def _fold(v, op):
    out = v[:, :LANES]
    for j in range(1, v.shape[1] // LANES):
        out = op(out, v[:, j * LANES : (j + 1) * LANES])
    return out


def first_kernel(chunks, tok_hbm, keys_hbm, tok, logits, dispatch, packed, stat, keys, acc, sem):
    tokens, width = tok.shape
    half = width // 2
    step = tokens // chunks
    keys_copy = pltpu.make_async_copy(keys_hbm, keys, sem.at[chunks])
    keys_copy.start()
    copies = [
        pltpu.make_async_copy(
            tok_hbm.at[pl.ds(i * step, step)], tok.at[pl.ds(i * step, step)], sem.at[i]
        )
        for i in range(chunks)
    ]
    for c in copies:
        c.start()
    other = pl.multiple_of((1 - _core()) * half, LANES)
    keys_copy.wait()
    keys_t = keys[...].T

    def weigh(i):
        return jnp.dot(
            dispatch[:, i * step : (i + 1) * step],
            tok[i * step : (i + 1) * step, pl.ds(other, half)],
            preferred_element_type=F32,
        )

    peaks, total = [], None
    for i in range(chunks):
        copies[i].wait()
        part = lax.dot_general(
            keys_t,
            tok[i * step : (i + 1) * step, :],
            (((1,), (1,)), ((), ())),
            preferred_element_type=F32,
        )
        logits[:, i * step : (i + 1) * step] = part
        peak = _wide(jnp.max(_fold(part, jnp.maximum), axis=1, keepdims=True))
        if i:
            peak = jnp.maximum(peak, peaks[-1])
        e = jnp.concatenate(
            [jnp.exp(part[:, j : j + LANES] - peak) for j in range(0, step, LANES)], axis=1
        )
        if i == 1:
            acc[...] = _times(weigh(0), jnp.exp(peaks[0] - peak))
        elif i > 1:
            acc[...] = _times(acc[...] + weigh(i - 1), jnp.exp(peaks[-1] - peak))
        dispatch[:, i * step : (i + 1) * step] = e.astype(BF16)
        add = _fold(e, jnp.add)
        total = add if i == 0 else total * jnp.exp(peaks[-1] - peak) + add
        peaks.append(peak)
    total = _wide(jnp.sum(total, axis=1, keepdims=True))
    sums = acc[...] + weigh(chunks - 1)
    packed[:, :half] = sums.astype(BF16)
    packed[:, half:] = _pieces(peak, total)
    stat[:, :LANES] = peak
    stat[:, LANES : 2 * LANES] = total
    for i in range(chunks):
        stat[:, (2 + i) * LANES : (3 + i) * LANES] = jnp.exp(peaks[i] - peak)


def own_kernel(chunks, tok, dispatch, stat, own):
    half = tok.shape[1] // 2
    step = tok.shape[0] // chunks
    off = pl.multiple_of(_core() * half, LANES)
    sums = None
    for i in range(chunks):
        part = _times(
            jnp.dot(
                dispatch[:, i * step : (i + 1) * step],
                tok[i * step : (i + 1) * step, pl.ds(off, half)],
                preferred_element_type=F32,
            ),
            stat[:, (2 + i) * LANES : (3 + i) * LANES],
        )
        sums = part if sums is None else sums + part
    own[...] = sums


def combine_kernel(after, logits, w_in_hbm, w_out_hbm, combine, w_in, w_out, sem):
    copies = [
        pltpu.make_async_copy(w_in_hbm, w_in, sem.at[0]),
        pltpu.make_async_copy(w_out_hbm, w_out, sem.at[1]),
    ]
    for c in copies:
        c.start()
    v = logits[...]
    e = jnp.exp(v - jnp.max(v, axis=0, keepdims=True))
    combine[...] = (e / jnp.sum(e, axis=0, keepdims=True)).astype(BF16).T
    for c in copies:
        c.wait()


def expert_kernel(slot_own, slot_other, w_in, w_out, own, send):
    half = slot_own.shape[1]
    mine = pl.multiple_of(_core() * half, LANES)
    other = pl.multiple_of((1 - _core()) * half, LANES)
    hidden = jnp.dot(slot_own[...], w_in[pl.ds(mine, half), :], preferred_element_type=F32)
    hidden += jnp.dot(slot_other[...], w_in[pl.ds(other, half), :], preferred_element_type=F32)
    hidden = jax.nn.gelu(hidden).astype(BF16)
    send[...] = jnp.dot(hidden, w_out[:, pl.ds(other, half)], preferred_element_type=F32)
    own[...] = jnp.dot(hidden, w_out[:, pl.ds(mine, half)], preferred_element_type=F32)


def core_merge_kernel(own, stat, got, keep, keep_stat, send1, send2, send3):
    rows, half = keep.shape
    for k, ref in enumerate((keep, send1, send2, send3)):
        part = pl.ds(pl.multiple_of(lax.rem(_y() + k, 4) * rows, rows), rows)
        sums, peak, total = _merge(
            [
                (own[part, :], stat[part, :LANES], stat[part, LANES : 2 * LANES]),
                (got[part, :half].astype(F32), *_unpieces(got[part, half:])),
            ]
        )
        ref[:, :half] = sums.astype(ref.dtype)
        if k == 0:
            keep_stat[:, :LANES] = peak
            keep_stat[:, LANES:] = total
        else:
            ref[:, half:] = _pieces(peak, total)


def y_merge_kernel(after, own, stat, got1, got2, got3, keep, send1, send2, send3):
    rows, half = keep.shape[0], own.shape[1]
    for k, ref in enumerate((keep, send1, send2, send3)):
        part = pl.ds(pl.multiple_of(lax.rem(_z() + k, 4) * rows, rows), rows)
        sums, peak, total = _merge(
            [(own[part, :], stat[part, :LANES], stat[part, LANES:])]
            + [
                (g[part, :half].astype(F32), *_unpieces(g[part, half:]))
                for g in (got1, got2, got3)
            ]
        )
        ref[:, :half] = sums
        ref[:, half:] = _pair(peak, total)


def z_merge_kernel(own, got1, got2, got3, out):
    half = own.shape[1] - LANES
    sums, peak, total = _merge(
        [(g[:, :half], *_unpair(g[:, half:])) for g in (own, got1, got2, got3)]
    )
    out[:, :half] = sums
    out[:, half:] = _pair(peak, total)


def x_merge_kernel(own, got1, got2, got3, out):
    half = own.shape[1] - LANES
    sums, _, total = _merge(
        [(g[:, :half], *_unpair(g[:, half:])) for g in (own, got1, got2, got3)]
    )
    out[...] = (sums / _wide_as(total, half)).astype(BF16)


def _wide_as(v, width):
    return jnp.concatenate([v] * (width // LANES), axis=1)


def mix_kernel(chunks, own, combine, slot_out, *refs):
    out_hbm, buf, sem = refs[-3:]
    half = slot_out.shape[1]
    step = combine.shape[0] // chunks
    column = pl.multiple_of((_core() if own else 1 - _core()) * half, LANES)
    copies = []
    for i in range(chunks):
        buf[i] = jnp.dot(
            combine[i * step : (i + 1) * step, :], slot_out[...], preferred_element_type=F32
        ).astype(BF16)
        c = pltpu.make_async_copy(
            buf.at[i], out_hbm.at[pl.ds(i * step, step), pl.ds(column, half)], sem.at[i]
        )
        c.start()
        copies.append(c)
    for c in copies:
        c.wait()


def body(tokens, slot_keys, w_in, w_out):
    y, z = _y(), _z()

    tok, logits, dispatch, packed, stat = first(tokens, slot_keys)
    got = lax.ppermute(packed, "seq", _core_perm())
    own = own_sums(tok, dispatch, stat)

    own, stat, *send = core_merge(own, stat, got)
    got = [lax.ppermute(v, ("seq", "exp"), _y_perm(k + 1)) for k, v in enumerate(send)]
    combine, w_in, w_out = combine_weights(own, logits, w_in[0], w_out[0])
    own, *send = y_merge(combine, own, stat, *got)
    got = [lax.ppermute(v, "exp", _z_perm(k + 1)) for k, v in enumerate(send)]
    own = z_merge(own, *got)
    got = [lax.ppermute(own, "seq", _x_perm(k)) for k in range(1, 4)]
    slot_half = x_merge(own, *got)
    got = lax.ppermute(slot_half, "seq", _core_perm())
    mine, other = expert(slot_half, got, w_in, w_out)
    part = mine + lax.ppermute(other, "seq", _core_perm())
    whole = part + sum(lax.ppermute(part, "seq", _x_perm(k)) for k in range(1, 4))
    out = whole.astype(BF16)

    def gather(block, index, axes, perm):
        n = block.shape[0]
        res = jnp.zeros((4 * n, block.shape[1]), block.dtype)
        blocks = [block] + [lax.ppermute(block, axes, perm(k)) for k in range(1, 4)]
        for k, g in enumerate(blocks):
            res = lax.dynamic_update_slice_in_dim(res, g, ((index - k) % 4) * n, 0)
        return res

    out = gather(out, z, "exp", _z_perm)
    out = gather(out, y, ("seq", "exp"), _y_perm)
    other = lax.ppermute(out, "seq", _core_perm())
    mixed = mix(combine, out)
    return mix(combine, other, mixed)


CHUNKS = 4


def first(tokens, slot_keys):
    count, width = tokens.shape
    slots = slot_keys.shape[1]
    half = width // 2
    return _call(
        functools.partial(first_kernel, CHUNKS),
        "logits_and_sums",
        [
            pltpu.VMEM((count, width), BF16),
            pltpu.VMEM((slots, count), F32),
            pltpu.VMEM((slots, count), BF16),
            pltpu.VMEM((slots, half + LANES), BF16),
            pltpu.VMEM((slots, (2 + CHUNKS) * LANES), F32),
        ],
        [ANY, ANY],
        [
            pltpu.VMEM((width, slots), BF16),
            pltpu.VMEM((slots, half), F32),
            pltpu.SemaphoreType.DMA((CHUNKS + 1,)),
        ],
        vmem=16,
        flops=3 * count * slots * width,
        bytes_accessed=2 * count * width,
    )(*(pltpu.with_memory_space_constraint(v, pltpu.HBM) for v in (tokens, slot_keys)))


def own_sums(tok, dispatch, stat):
    return _call(
        functools.partial(own_kernel, CHUNKS),
        "own_sums",
        pltpu.VMEM((stat.shape[0], tok.shape[1] // 2), F32),
        [VMEM, VMEM, VMEM],
        vmem=12,
        flops=dispatch.size * tok.shape[1],
    )(tok, dispatch, stat)


def combine_weights(after, logits, w_in, w_out):
    slots, count = logits.shape
    return _call(
        combine_kernel,
        "combine",
        [
            pltpu.VMEM((count, slots), BF16),
            pltpu.VMEM(w_in.shape, BF16),
            pltpu.VMEM(w_out.shape, BF16),
        ],
        [ANY, VMEM, ANY, ANY],
        [pltpu.SemaphoreType.DMA((2,))],
        vmem=12,
        flops=10 * count * slots,
        bytes_accessed=4 * w_in.size,
    )(after, logits, *(pltpu.with_memory_space_constraint(v, pltpu.HBM) for v in (w_in, w_out)))


def expert(slot_own, slot_other, w_in, w_out):
    return _call(
        expert_kernel,
        "expert",
        [pltpu.VMEM(slot_own.shape, F32)] * 2,
        [VMEM] * 4,
        flops=4 * slot_own.shape[0] * w_in.size,
    )(slot_own, slot_other, w_in, w_out)


def core_merge(own, stat, got):
    rows, half = own.shape[0] // 4, own.shape[1]
    return _call(
        core_merge_kernel,
        "core_merge",
        [pltpu.VMEM((rows, half), F32), pltpu.VMEM((rows, 2 * LANES), F32)]
        + [pltpu.VMEM((rows, half + LANES), BF16)] * 3,
        [VMEM] * 3,
    )(own, stat, got)


def y_merge(after, own, stat, *got):
    rows, half = own.shape[0] // 4, own.shape[1]
    return _call(
        y_merge_kernel,
        "y_merge",
        [pltpu.VMEM((rows, half + LANES), F32)] * 4,
        [ANY] + [VMEM] * 5,
    )(after, own, stat, *got)


def z_merge(own, *got):
    return _call(z_merge_kernel, "z_merge", pltpu.VMEM(own.shape, F32), [VMEM] * 4)(own, *got)


def x_merge(own, *got):
    out = pltpu.VMEM((own.shape[0], own.shape[1] - LANES), BF16)
    return _call(x_merge_kernel, "x_merge", out, [VMEM] * 4)(own, *got)


def mix(combine, slot_out, *mixed):
    count, slots = combine.shape
    half = slot_out.shape[1]
    steps = 8
    return _call(
        functools.partial(mix_kernel, steps, not mixed),
        "mix",
        jax.ShapeDtypeStruct((count, 2 * half), BF16),
        [VMEM, VMEM] + [ANY] * len(mixed),
        [pltpu.VMEM((steps, count // steps, half), BF16), pltpu.SemaphoreType.DMA((steps,))],
        out_specs=ANY,
        vmem=12,
        flops=2 * count * slots * half,
        bytes_accessed=2 * count * half,
        input_output_aliases={2: 0} if mixed else {},
    )(combine, slot_out, *mixed)


def solution(mesh):
    return jax.shard_map(
        body,
        mesh=mesh,
        in_specs=(P(("dp", "seq", "exp"), None), P(), P("exp", None, "seq"), P("exp", "seq", None)),
        out_specs=P(("dp", "seq", "exp"), None),
        check_vma=False,
    )
```

```python
import functools

import jax
import jax.numpy as jnp
from jax import lax
from jax.experimental import pallas as pl
from jax.experimental.pallas import tpu as pltpu
from jax.sharding import PartitionSpec as P

F32 = jnp.float32
BF16 = jnp.bfloat16
LANES = 128
VMEM = pl.BlockSpec(memory_space=pltpu.VMEM)
ANY = pl.BlockSpec(memory_space=pl.ANY)


def _core():
    seq = lax.axis_index("seq")
    return lax.rem(seq + lax.div(seq, 2) + _y() + _z(), 2)


def _y():
    return lax.div(lax.axis_index("exp"), 4)


def _z():
    return lax.rem(lax.axis_index("exp"), 4)


def _core_perm():
    return [(s, s ^ 1) for s in range(8)]


def _x_perm(k):
    return [(s, ((s // 2 + k) % 4) * 2 + (s + k) % 2) for s in range(8)]


def _y_perm(k):
    return [
        (s * 16 + e, (s ^ (k & 1)) * 16 + ((e // 4 + k) % 4) * 4 + e % 4)
        for s in range(8)
        for e in range(16)
    ]


def _z_perm(k):
    return [
        (s * 16 + e, (s ^ (k & 1)) * 16 + (e // 4) * 4 + (e % 4 + k) % 4)
        for s in range(8)
        for e in range(16)
    ]


def _call(kernel, name, out_shape, in_specs, scratch=(), out_specs=None, vmem=6, flops=0, bytes_accessed=0, **kw):
    many = isinstance(out_shape, list)
    if out_specs is None:
        out_specs = [VMEM] * len(out_shape) if many else VMEM
    return pl.pallas_call(
        kernel,
        in_specs=in_specs,
        out_specs=out_specs,
        out_shape=out_shape,
        scratch_shapes=list(scratch),
        compiler_params=pltpu.CompilerParams(vmem_limit_bytes=vmem << 20),
        cost_estimate=pl.CostEstimate(flops=flops, bytes_accessed=bytes_accessed, transcendentals=0),
        name=name,
        **kw,
    )


def _lane(n):
    return lax.broadcasted_iota(jnp.int32, (n, LANES), 1)


def _wide(v):
    return jnp.broadcast_to(v, (v.shape[0], LANES))


def _pieces(peak, total):
    lane = _lane(peak.shape[0])
    st = jnp.zeros(peak.shape, F32)
    j = 0
    for v in (peak, total):
        for _ in range(3):
            p = v.astype(BF16).astype(F32)
            st = jnp.where(lane == j, p, st)
            v = v - p
            j += 1
    return st.astype(BF16)


def _unpieces(st):
    row = lax.broadcasted_iota(jnp.int32, (LANES, 2 * LANES), 0)
    column = lax.broadcasted_iota(jnp.int32, (LANES, 2 * LANES), 1)
    first = jnp.where(column < LANES, 0, 3)
    pick = jnp.where((row >= first) & (row < first + 3), 1.0, 0.0).astype(BF16)
    both = jnp.dot(st, pick, preferred_element_type=F32)
    return both[:, :LANES], both[:, LANES:]


def _pair(peak, total):
    lane = _lane(peak.shape[0])
    return jnp.where(lane == 0, peak, jnp.where(lane == 1, total, 0.0))


def _unpair(st):
    return _wide(st[:, 0:1]), _wide(st[:, 1:2])


def _times(v, scale):
    return jnp.concatenate(
        [v[:, j : j + LANES] * scale for j in range(0, v.shape[1], LANES)], axis=1
    )


def _merge(parts):
    peak = parts[0][1]
    for _, p, _ in parts[1:]:
        peak = jnp.maximum(peak, p)
    sums, total = None, None
    for s, p, t in parts:
        a = jnp.exp(p - peak)
        sums = _times(s, a) if sums is None else sums + _times(s, a)
        total = t * a if total is None else total + t * a
    return sums, peak, total


def _fold(v, op):
    out = v[:, :LANES]
    for j in range(1, v.shape[1] // LANES):
        out = op(out, v[:, j * LANES : (j + 1) * LANES])
    return out


def first_kernel(chunks, tok_hbm, keys_hbm, tok, logits, dispatch, packed, stat, keys, acc, sem):
    tokens, width = tok.shape
    half = width // 2
    step = tokens // chunks
    keys_copy = pltpu.make_async_copy(keys_hbm, keys, sem.at[chunks])
    keys_copy.start()
    copies = [
        pltpu.make_async_copy(
            tok_hbm.at[pl.ds(i * step, step)], tok.at[pl.ds(i * step, step)], sem.at[i]
        )
        for i in range(chunks)
    ]
    for c in copies:
        c.start()
    other = pl.multiple_of((1 - _core()) * half, LANES)
    keys_copy.wait()
    keys_t = keys[...].T

    def weigh(i):
        return jnp.dot(
            dispatch[:, i * step : (i + 1) * step],
            tok[i * step : (i + 1) * step, pl.ds(other, half)],
            preferred_element_type=F32,
        )

    peaks, total = [], None
    for i in range(chunks):
        copies[i].wait()
        part = lax.dot_general(
            keys_t,
            tok[i * step : (i + 1) * step, :],
            (((1,), (1,)), ((), ())),
            preferred_element_type=F32,
        )
        logits[:, i * step : (i + 1) * step] = part
        peak = _wide(jnp.max(_fold(part, jnp.maximum), axis=1, keepdims=True))
        if i:
            peak = jnp.maximum(peak, peaks[-1])
        e = jnp.concatenate(
            [jnp.exp(part[:, j : j + LANES] - peak) for j in range(0, step, LANES)], axis=1
        )
        if i == 1:
            acc[...] = _times(weigh(0), jnp.exp(peaks[0] - peak))
        elif i > 1:
            acc[...] = _times(acc[...] + weigh(i - 1), jnp.exp(peaks[-1] - peak))
        dispatch[:, i * step : (i + 1) * step] = e.astype(BF16)
        add = _fold(e, jnp.add)
        total = add if i == 0 else total * jnp.exp(peaks[-1] - peak) + add
        peaks.append(peak)
    total = _wide(jnp.sum(total, axis=1, keepdims=True))
    sums = acc[...] + weigh(chunks - 1)
    packed[:, :half] = sums.astype(BF16)
    packed[:, half:] = _pieces(peak, total)
    stat[:, :LANES] = peak
    stat[:, LANES : 2 * LANES] = total
    for i in range(chunks):
        stat[:, (2 + i) * LANES : (3 + i) * LANES] = jnp.exp(peaks[i] - peak)


def own_kernel(chunks, tok, dispatch, stat, own):
    half = tok.shape[1] // 2
    step = tok.shape[0] // chunks
    off = pl.multiple_of(_core() * half, LANES)
    sums = None
    for i in range(chunks):
        part = _times(
            jnp.dot(
                dispatch[:, i * step : (i + 1) * step],
                tok[i * step : (i + 1) * step, pl.ds(off, half)],
                preferred_element_type=F32,
            ),
            stat[:, (2 + i) * LANES : (3 + i) * LANES],
        )
        sums = part if sums is None else sums + part
    own[...] = sums


def combine_kernel(after, logits, w_in_hbm, w_out_hbm, combine, w_in, w_out, sem):
    copies = [
        pltpu.make_async_copy(w_in_hbm, w_in, sem.at[0]),
        pltpu.make_async_copy(w_out_hbm, w_out, sem.at[1]),
    ]
    for c in copies:
        c.start()
    v = logits[...]
    e = jnp.exp(v - jnp.max(v, axis=0, keepdims=True))
    combine[...] = (e / jnp.sum(e, axis=0, keepdims=True)).astype(BF16).T
    for c in copies:
        c.wait()


def expert_kernel(slot_own, slot_other, w_in, w_out, own, send):
    half = slot_own.shape[1]
    mine = pl.multiple_of(_core() * half, LANES)
    other = pl.multiple_of((1 - _core()) * half, LANES)
    hidden = jnp.dot(slot_own[...], w_in[pl.ds(mine, half), :], preferred_element_type=F32)
    hidden += jnp.dot(slot_other[...], w_in[pl.ds(other, half), :], preferred_element_type=F32)
    hidden = jax.nn.gelu(hidden).astype(BF16)
    send[...] = jnp.dot(hidden, w_out[:, pl.ds(other, half)], preferred_element_type=F32)
    own[...] = jnp.dot(hidden, w_out[:, pl.ds(mine, half)], preferred_element_type=F32)


def core_merge_kernel(own, stat, got, keep, keep_stat, send1, send2, send3):
    rows, half = keep.shape
    for k, ref in enumerate((keep, send1, send2, send3)):
        part = pl.ds(pl.multiple_of(lax.rem(_y() + k, 4) * rows, rows), rows)
        sums, peak, total = _merge(
            [
                (own[part, :], stat[part, :LANES], stat[part, LANES : 2 * LANES]),
                (got[part, :half].astype(F32), *_unpieces(got[part, half:])),
            ]
        )
        ref[:, :half] = sums.astype(ref.dtype)
        if k == 0:
            keep_stat[:, :LANES] = peak
            keep_stat[:, LANES:] = total
        else:
            ref[:, half:] = _pieces(peak, total)


def y_merge_kernel(after, own, stat, got1, got2, got3, keep, send1, send2, send3):
    rows, half = keep.shape[0], own.shape[1]
    for k, ref in enumerate((keep, send1, send2, send3)):
        part = pl.ds(pl.multiple_of(lax.rem(_z() + k, 4) * rows, rows), rows)
        sums, peak, total = _merge(
            [(own[part, :], stat[part, :LANES], stat[part, LANES:])]
            + [
                (g[part, :half].astype(F32), *_unpieces(g[part, half:]))
                for g in (got1, got2, got3)
            ]
        )
        ref[:, :half] = sums
        ref[:, half:] = _pair(peak, total)


def z_merge_kernel(own, got1, got2, got3, out):
    half = own.shape[1] - LANES
    sums, peak, total = _merge(
        [(g[:, :half], *_unpair(g[:, half:])) for g in (own, got1, got2, got3)]
    )
    out[:, :half] = sums
    out[:, half:] = _pair(peak, total)


def x_merge_kernel(own, got1, got2, got3, out):
    half = own.shape[1] - LANES
    sums, _, total = _merge(
        [(g[:, :half], *_unpair(g[:, half:])) for g in (own, got1, got2, got3)]
    )
    out[...] = (sums / _wide_as(total, half)).astype(BF16)


def _wide_as(v, width):
    return jnp.concatenate([v] * (width // LANES), axis=1)


def mix_kernel(chunks, own, combine, slot_out, *refs):
    out_hbm, buf, sem = refs[-3:]
    half = slot_out.shape[1]
    step = combine.shape[0] // chunks
    column = pl.multiple_of((_core() if own else 1 - _core()) * half, LANES)
    copies = []
    for i in range(chunks):
        buf[i] = jnp.dot(
            combine[i * step : (i + 1) * step, :], slot_out[...], preferred_element_type=F32
        ).astype(BF16)
        c = pltpu.make_async_copy(
            buf.at[i], out_hbm.at[pl.ds(i * step, step), pl.ds(column, half)], sem.at[i]
        )
        c.start()
        copies.append(c)
    for c in copies:
        c.wait()


def body(tokens, slot_keys, w_in, w_out):
    y, z = _y(), _z()

    tok, logits, dispatch, packed, stat = first(tokens, slot_keys)
    got = lax.ppermute(packed, "seq", _core_perm())
    own = own_sums(tok, dispatch, stat)

    own, stat, *send = core_merge(own, stat, got)
    got = [lax.ppermute(v, ("seq", "exp"), _y_perm(k + 1)) for k, v in enumerate(send)]
    combine, w_in, w_out = combine_weights(own, logits, w_in[0], w_out[0])
    own, *send = y_merge(combine, own, stat, *got)
    got = [lax.ppermute(v, ("seq", "exp"), _z_perm(k + 1)) for k, v in enumerate(send)]
    own = z_merge(own, *got)
    got = [lax.ppermute(own, "seq", _x_perm(k)) for k in range(1, 4)]
    slot_half = x_merge(own, *got)
    got = lax.ppermute(slot_half, "seq", _core_perm())
    mine, other = expert(slot_half, got, w_in, w_out)
    part = mine + lax.ppermute(other, "seq", _core_perm())
    whole = part + sum(lax.ppermute(part, "seq", _x_perm(k)) for k in range(1, 4))
    out = whole.astype(BF16)

    def gather(block, index, perm):
        n = block.shape[0]
        res = jnp.zeros((4 * n, block.shape[1]), block.dtype)
        blocks = [block] + [lax.ppermute(block, ("seq", "exp"), perm(k)) for k in range(1, 4)]
        for k, g in enumerate(blocks):
            res = lax.dynamic_update_slice_in_dim(res, g, ((index - k) % 4) * n, 0)
        return res

    out = gather(out, z, _z_perm)
    out = gather(out, y, _y_perm)
    other = lax.ppermute(out, "seq", _core_perm())
    mixed = mix(combine, out)
    return mix(combine, other, mixed)


CHUNKS = 4


def first(tokens, slot_keys):
    count, width = tokens.shape
    slots = slot_keys.shape[1]
    half = width // 2
    return _call(
        functools.partial(first_kernel, CHUNKS),
        "logits_and_sums",
        [
            pltpu.VMEM((count, width), BF16),
            pltpu.VMEM((slots, count), F32),
            pltpu.VMEM((slots, count), BF16),
            pltpu.VMEM((slots, half + LANES), BF16),
            pltpu.VMEM((slots, (2 + CHUNKS) * LANES), F32),
        ],
        [ANY, ANY],
        [
            pltpu.VMEM((width, slots), BF16),
            pltpu.VMEM((slots, half), F32),
            pltpu.SemaphoreType.DMA((CHUNKS + 1,)),
        ],
        vmem=16,
        flops=3 * count * slots * width,
        bytes_accessed=2 * count * width,
    )(*(pltpu.with_memory_space_constraint(v, pltpu.HBM) for v in (tokens, slot_keys)))


def own_sums(tok, dispatch, stat):
    return _call(
        functools.partial(own_kernel, CHUNKS),
        "own_sums",
        pltpu.VMEM((stat.shape[0], tok.shape[1] // 2), F32),
        [VMEM, VMEM, VMEM],
        vmem=12,
        flops=dispatch.size * tok.shape[1],
    )(tok, dispatch, stat)


def combine_weights(after, logits, w_in, w_out):
    slots, count = logits.shape
    return _call(
        combine_kernel,
        "combine",
        [
            pltpu.VMEM((count, slots), BF16),
            pltpu.VMEM(w_in.shape, BF16),
            pltpu.VMEM(w_out.shape, BF16),
        ],
        [ANY, VMEM, ANY, ANY],
        [pltpu.SemaphoreType.DMA((2,))],
        vmem=12,
        flops=10 * count * slots,
        bytes_accessed=4 * w_in.size,
    )(after, logits, *(pltpu.with_memory_space_constraint(v, pltpu.HBM) for v in (w_in, w_out)))


def expert(slot_own, slot_other, w_in, w_out):
    return _call(
        expert_kernel,
        "expert",
        [pltpu.VMEM(slot_own.shape, F32)] * 2,
        [VMEM] * 4,
        flops=4 * slot_own.shape[0] * w_in.size,
    )(slot_own, slot_other, w_in, w_out)


def core_merge(own, stat, got):
    rows, half = own.shape[0] // 4, own.shape[1]
    return _call(
        core_merge_kernel,
        "core_merge",
        [pltpu.VMEM((rows, half), F32), pltpu.VMEM((rows, 2 * LANES), F32)]
        + [pltpu.VMEM((rows, half + LANES), BF16)] * 3,
        [VMEM] * 3,
    )(own, stat, got)


def y_merge(after, own, stat, *got):
    rows, half = own.shape[0] // 4, own.shape[1]
    return _call(
        y_merge_kernel,
        "y_merge",
        [pltpu.VMEM((rows, half + LANES), F32)] * 4,
        [ANY] + [VMEM] * 5,
    )(after, own, stat, *got)


def z_merge(own, *got):
    return _call(z_merge_kernel, "z_merge", pltpu.VMEM(own.shape, F32), [VMEM] * 4)(own, *got)


def x_merge(own, *got):
    out = pltpu.VMEM((own.shape[0], own.shape[1] - LANES), BF16)
    return _call(x_merge_kernel, "x_merge", out, [VMEM] * 4)(own, *got)


def mix(combine, slot_out, *mixed):
    count, slots = combine.shape
    half = slot_out.shape[1]
    steps = 8
    return _call(
        functools.partial(mix_kernel, steps, not mixed),
        "mix",
        jax.ShapeDtypeStruct((count, 2 * half), BF16),
        [VMEM, VMEM] + [ANY] * len(mixed),
        [pltpu.VMEM((steps, count // steps, half), BF16), pltpu.SemaphoreType.DMA((steps,))],
        out_specs=ANY,
        vmem=12,
        flops=2 * count * slots * half,
        bytes_accessed=2 * count * half,
        input_output_aliases={2: 0} if mixed else {},
    )(combine, slot_out, *mixed)


def solution(mesh):
    return jax.shard_map(
        body,
        mesh=mesh,
        in_specs=(P(("dp", "seq", "exp"), None), P(), P("exp", None, "seq"), P("exp", "seq", None)),
        out_specs=P(("dp", "seq", "exp"), None),
        check_vma=False,
    )
```
